32 devices in a mesh: groups: 2 (over y), dp: 4 (over z), tensor: 4 (over x, core).
Axes of the slice: x: 2, y: 2, z: 4, core: 2. Of those that a mesh axis runs over, the one named last changes fastest.
Arguments:
- inputs: bfloat16 [3, 32, 12288], P(None, ('groups', 'dp')), parts along dimension 1, may hold values from -6 to 6
- ln_gain: float32 [12288], replicated, may hold values from 0.1 to 1.9
- w_qkv: bfloat16 [3, 24, 12288, 128], P(None, 'tensor', 'dp'), may hold values from -0.0546875 to 0.0546875
- w_out: bfloat16 [24, 128, 12288], P('tensor', None, 'dp'), may hold values from -0.375 to 0.375
- key_cache: bfloat16 [32, 24, 128, 128], P(('groups', 'dp'), 'tensor'), parts along dimension 0, may hold values from -48 to 48
- value_cache: bfloat16 [32, 24, 128, 128], P(('groups', 'dp'), 'tensor'), parts along dimension 0, may hold values from -6 to 6
- cache_lens: int32 [32], P(('groups', 'dp')), parts along dimension 0, may hold values from 1 to 128, as said below
- active_heads: int32 [6, 8], P('groups'), parts along dimension 0, may hold values from 0 to 23, as said below
Outputs:
- attended: bfloat16 [3, 32, 12288], P(None, 'groups', ('dp', 'tensor')), parts along dimension 1
The draws below stay inside these ranges and needn't reach their ends.
There are 2 independent parts, one for each index of `groups`. The reference program is written for one: setup_inputs(seed, part) draws one part's arguments, and reference() takes and returns one part's arrays. A program takes and returns all parts, laid end to end along the dimension named above; an argument that names none is the same for every part. Nothing has to cross between parts.
Inputs may be any that keep to these rules, and one draw needn't show every extreme that they name: `active_heads`: each step lists 8 distinct heads in increasing order; each aligned block of 6 heads holds at most 4 of them, and in every step some block holds exactly 4. `cache_lens`: some row has exactly 128 cached positions.
All inputs are finite; a program needn't handle non-finite values.
Results may differ from the reference program's by a relative error of at most 0.012.
The reference program's roundings to bfloat16 on the way count: a program that leaves them out, or rounds other values in their place, can miss the bound.
Values may be sent and summed in bfloat16 or wider, within the bound.
A program may use at most 64 MiB of HBM per device.

```python
import jax
import jax.numpy as jnp
from jax import lax

D = 12288
HEAD_DIM = 128
HEADS_DEV = 6
STEPS = 3
CACHE = 128
HEADS = 24
ACTIVE = 8
ROWS = 16


def draw_key_cache(key, part):
    key = jax.random.fold_in(key, 11)
    normal_key = jax.random.fold_in(key, 0)
    shape_all = (ROWS, HEADS, CACHE, HEAD_DIM)
    base = jax.random.normal(normal_key, shape_all, jnp.float32)
    base = jnp.clip(base, -6.0, 6.0)
    return base.astype(jnp.bfloat16)


def draw_cache_lens(key, part):
    key = jax.random.fold_in(key, 12)
    length_key, pick_key = jax.random.split(key)
    lengths = jax.random.randint(length_key, (ROWS,), 1, CACHE + 1, dtype=jnp.int32)
    longest = jax.random.randint(pick_key, (), 0, ROWS, dtype=jnp.int32)
    return lengths.at[longest].set(CACHE)


def draw_active_heads(key, part):
    key = jax.random.fold_in(key, 13)
    block_count = HEADS // HEADS_DEV

    def one_step(step_key):
        first_key, second_key, order_key = jax.random.split(step_key, 3)
        busiest = jax.random.randint(first_key, (), 0, block_count, dtype=jnp.int32)
        emptied = (busiest + 1 + jax.random.randint(second_key, (), 0, block_count - 1, dtype=jnp.int32)) % block_count
        block_ids = jnp.arange(block_count, dtype=jnp.int32)
        quota = 2 + 2 * (block_ids == busiest).astype(jnp.int32) - 2 * (block_ids == emptied).astype(jnp.int32)
        order_keys = jax.random.split(order_key, block_count)
        ranks = jax.vmap(lambda k: jax.random.permutation(k, HEADS_DEV))(order_keys).astype(jnp.int32)
        chosen = (ranks < quota[:, None]).reshape(-1)
        ranking = jnp.where(chosen, 0, HEADS) + jnp.arange(HEADS, dtype=jnp.int32)
        return jnp.argsort(ranking)[:ACTIVE].astype(jnp.int32)
    return jax.vmap(one_step)(jax.random.split(key, STEPS))


def block_levels(key, extent, pieces, least, top_value):
    def one(dim, parts):
        heights = jax.random.uniform(jax.random.fold_in(jax.random.fold_in(key, 6), dim), (parts,), jnp.float32, least / len(pieces), top_value / len(pieces))
        return jnp.repeat(jnp.exp(heights), extent[dim] // parts).reshape((-1,) + (1,) * (len(extent) - dim - 1))

    factor_of = one(*pieces[0])
    for cut in pieces[1:]:
        factor_of = factor_of * one(*cut)
    return factor_of


def normal_values(key, dims, scale, limit, cuts=(), kind=jnp.bfloat16):
    entries = scale * jax.random.normal(key, dims, jnp.float32)
    if cuts:
        entries = entries * block_levels(key, dims, cuts, -0.22, 0.18)
    return jnp.clip(entries, -limit, limit).astype(kind)


def setup_inputs(seed: int = 0, part: int = 0) -> dict:
    seeds = jax.random.split(jax.random.key(seed), 9)
    part_keys = jax.random.split(jax.random.fold_in(seeds[8], part), 9)
    return {
        "inputs": normal_values(part_keys[0], (STEPS, ROWS, D), 1.0, 6.0, ((1, 4),)),
        "ln_gain": jnp.clip(1.0 + 0.18 * jax.random.normal(seeds[1], (D,), jnp.float32), 0.1, 1.9),
        "w_qkv": normal_values(seeds[2], (3, HEADS, D, HEAD_DIM), D ** -0.5, 0.0546875, ((1, 4), (2, 4))),
        "w_out": normal_values(seeds[3], (HEADS, HEAD_DIM, D), (ACTIVE * HEAD_DIM // 4) ** -0.5, 0.375, ((0, 4), (2, 4))),
        "key_cache": draw_key_cache(jax.random.fold_in(jax.random.fold_in(seeds[8], part), 71), part),
        "value_cache": normal_values(part_keys[5], (ROWS, HEADS, CACHE, HEAD_DIM), 1.0, 6.0, ((0, 4), (1, 4))),
        "cache_lens": draw_cache_lens(jax.random.fold_in(jax.random.fold_in(seeds[8], part), 71), part),
        "active_heads": draw_active_heads(jax.random.fold_in(jax.random.fold_in(seeds[8], part), 71), part),
    }


def normalize(rows, gain):
    values = rows.astype(jnp.float32)
    center = values - lax.optimization_barrier(jnp.mean(values, axis=-1, keepdims=True))
    spread = lax.optimization_barrier(jnp.mean(center * center, axis=-1, keepdims=True))
    return (center * lax.rsqrt(spread + 1e-05) * gain).astype(jnp.bfloat16)

def attend(queries, step_now, picked, alive_slots, new_keys, new_values, live_table, key_cache, value_cache, cache_lens):
    scale = queries.shape[-1] ** (-0.5)
    cached_keys = jnp.take(key_cache, picked, axis=1).astype(jnp.float32)
    cached_values = jnp.take(value_cache, picked, axis=1).astype(jnp.float32)
    query_wide = queries.astype(jnp.float32)
    old_scores = jnp.einsum('bch,bcph->bcp', query_wide, cached_keys) * scale
    positions = jnp.arange(cached_keys.shape[2], dtype=jnp.int32)
    old_valid = positions[None, None, :] < cache_lens[:, None, None]
    fresh_keys = jnp.take(new_keys, picked, axis=2).astype(jnp.float32)
    fresh_values = jnp.take(new_values, picked, axis=2).astype(jnp.float32)
    fresh_scores = jnp.einsum('bch,jbch->bcj', query_wide, fresh_keys) * scale
    step_ids = jnp.arange(new_keys.shape[0], dtype=jnp.int32)
    fresh_valid = (step_ids <= step_now)[:, None] & jnp.take(live_table, picked, axis=1)
    fresh_valid = jnp.transpose(fresh_valid)[None, :, :]
    top_score = jnp.maximum(lax.optimization_barrier(jnp.max(jnp.where(old_valid, old_scores, -jnp.inf), axis=2)), lax.optimization_barrier(jnp.max(jnp.where(fresh_valid, fresh_scores, -jnp.inf), axis=2)))
    old_weight = jnp.where(old_valid, jnp.exp(old_scores - top_score[..., None]), 0.0)
    fresh_weight = jnp.where(fresh_valid, jnp.exp(fresh_scores - top_score[..., None]), 0.0)
    weight_sum = lax.optimization_barrier(jnp.sum(old_weight, axis=2)) + lax.optimization_barrier(jnp.sum(fresh_weight, axis=2))
    old_prob = (old_weight / weight_sum[..., None]).astype(jnp.bfloat16).astype(jnp.float32)
    fresh_prob = (fresh_weight / weight_sum[..., None]).astype(jnp.bfloat16).astype(jnp.float32)
    blended = jnp.einsum('bcp,bcph->bch', old_prob, cached_values) + jnp.einsum('bcj,jbch->bch', fresh_prob, fresh_values)
    blended = jnp.where(alive_slots[None, :, None], blended, 0.0)
    return blended.astype(jnp.bfloat16).reshape(queries.shape[0], -1)

def reference(inputs, ln_gain, w_qkv, w_out, key_cache, value_cache, cache_lens, active_heads):
    normed = normalize(inputs, ln_gain)
    head_ids = jnp.arange(HEADS, dtype=jnp.int32)
    live_table = jnp.any(active_heads[:, :, None] == head_ids[None, None, :], axis=1)
    new_keys = jnp.zeros((STEPS, ROWS, HEADS, HEAD_DIM), jnp.bfloat16)
    new_values = jnp.zeros((STEPS, ROWS, HEADS, HEAD_DIM), jnp.bfloat16)
    results = []
    for step_now in range(STEPS):
        chosen = active_heads[step_now].astype(jnp.int32)
        weights_now = jnp.transpose(jnp.take(w_qkv, chosen, axis=1), (2, 0, 1, 3)).reshape(D, -1)
        projected = jnp.dot(normed[step_now], weights_now, preferred_element_type=jnp.float32)
        projected = projected.astype(jnp.bfloat16).reshape(ROWS, 3, ACTIVE, HEAD_DIM)
        new_keys = new_keys.at[step_now].set(new_keys[step_now].at[:, chosen].set(projected[:, 1]))
        new_values = new_values.at[step_now].set(new_values[step_now].at[:, chosen].set(projected[:, 2]))
        alive_slots = jnp.ones((ACTIVE,), dtype=bool)
        blended = attend(projected[:, 0], step_now, chosen, alive_slots, new_keys, new_values, live_table, key_cache, value_cache, cache_lens)
        out_weights = jnp.take(w_out, chosen, axis=0).reshape(ACTIVE * HEAD_DIM, D)
        results.append(jnp.dot(blended, out_weights, preferred_element_type=jnp.float32).astype(jnp.bfloat16))
    return jnp.stack(results)
```

```python
import functools

import jax
import jax.numpy as jnp
import numpy as np
from jax import lax
from jax.experimental import pallas as pl
from jax.experimental.pallas import tpu as pltpu
from jax.sharding import PartitionSpec as P

HEAD_CAP = 4
TILE = 16
MESH = pl.DeviceIdType.MESH


def kernel(
    dims,
    x_ref,
    gain_ref,
    perm_ref,
    lens_ref,
    active_ref,
    wqkv_hbm,
    wout_hbm,
    kc_hbm,
    vc_hbm,
    out_ref,
    wq,
    wo,
    kc,
    vc,
    rows32,
    nsend,
    xg,
    raw,
    packed,
    psend,
    precv,
    mg,
    osend,
    orecv,
    w_sem,
    c_sem,
    s1,
    r1,
    s2,
    r2,
    s3,
    r3,
    s4,
    r4,
):
    ndp, nt, heads, steps, rows, direct = dims
    hd = wq.shape[3]
    feats = wq.shape[2]
    cache = kc.shape[2]
    caps = HEAD_CAP
    spare = heads - caps
    me = lax.axis_index("dp")
    mt = lax.axis_index("tensor")
    f32, bf16 = jnp.float32, jnp.bfloat16

    weight_copies = []
    for t in range(3):
        for pair in range(heads // 2):
            c = pltpu.make_async_copy(
                wqkv_hbm.at[t, pl.ds(2 * pair, 2)],
                wq.at[t, pl.ds(2 * pair, 2)],
                w_sem.at[t * (heads // 2) + pair],
            )
            c.start()
            weight_copies.append(c)
    late = [
        pltpu.make_async_copy(kc_hbm, kc, c_sem.at[0]),
        pltpu.make_async_copy(vc_hbm, vc, c_sem.at[1]),
        pltpu.make_async_copy(wout_hbm, wo, c_sem.at[2]),
    ]
    for c in late:
        c.start()

    barrier = pltpu.get_barrier_semaphore()
    for k in range(1, ndp):
        pl.semaphore_signal(
            barrier, inc=1, device_id={"dp": lax.rem(me + k, ndp)}, device_id_type=MESH
        )
    if direct:
        for k in range(1, nt):
            pl.semaphore_signal(
                barrier, inc=1, device_id={"tensor": lax.rem(mt + k, nt)}, device_id_type=MESH
            )

    total = x_ref.shape[2]
    if TILE > steps * rows:
        rows32[...] = jnp.zeros_like(rows32)
    for s in range(steps):
        v = x_ref[s].astype(f32)
        center = v - jnp.sum(v, axis=-1, keepdims=True) * (1.0 / total)
        spread = jnp.sum(center * center, axis=-1, keepdims=True) * (1.0 / total)
        rows32[rows * s : rows * (s + 1), :] = center * lax.rsqrt(spread + 1e-05) * gain_ref[...]
    for p in range(ndp):
        nsend[p] = rows32[:, p * feats : (p + 1) * feats].astype(bf16)

    pl.semaphore_wait(barrier, ndp - 1 + (nt - 1 if direct else 0))

    def dp_copy(k, src, dst, send, recv):
        return pltpu.make_async_remote_copy(
            src_ref=src,
            dst_ref=dst,
            send_sem=send,
            recv_sem=recv,
            device_id={"dp": lax.rem(me + k, ndp)},
            device_id_type=MESH,
        )

    first = []
    for k in range(1, ndp):
        c = dp_copy(k, nsend.at[lax.rem(me + k, ndp)], xg.at[me], s1.at[k - 1], r1.at[k - 1])
        c.start()
        first.append(c)
    xg[me] = nsend[me]

    row = lax.broadcasted_iota(jnp.int32, (TILE, hd), 0)
    step_is = [(row >= rows * s) & (row < rows * (s + 1)) for s in range(steps)]
    row_is = []
    for r in range(rows):
        m = row == r
        for s in range(1, steps):
            m = m | (row == rows * s + r)
        row_is.append(m)
    live = []
    slot_of = []
    for s in range(steps):
        ids = [active_ref[s, a] for a in range(active_ref.shape[1])]
        flags, ranks = [], []
        seen = jnp.int32(0)
        for h in range(heads):
            hid = mt * heads + h
            f = jnp.int32(0)
            for i in ids:
                f = f + jnp.where(i == hid, jnp.int32(1), jnp.int32(0))
            flags.append(f)
            ranks.append(jnp.where(f > 0, jnp.maximum(seen, h - spare), jnp.int32(-1)))
            seen = seen + f
        live.append(flags)
        slot_of.append(ranks)
    rank_rows = []
    for h in range(heads):
        v = jnp.full((TILE, hd), -1, jnp.int32)
        for s in range(steps):
            v = jnp.where(step_is[s], slot_of[s][h], v)
        rank_rows.append(v)
    len_rows = jnp.full((TILE, cache), cache, jnp.int32)
    for r in range(rows):
        len_rows = jnp.where(row_is[r], lens_ref[r], len_rows)
    old_valid = lax.broadcasted_iota(jnp.int32, (TILE, cache), 1) < len_rows
    qrow = lax.broadcasted_iota(jnp.int32, (TILE, TILE), 0)
    kcol = lax.broadcasted_iota(jnp.int32, (TILE, TILE), 1)
    same = qrow == kcol
    for d in range(1, steps):
        same = same | (qrow - kcol == rows * d)
    same = same & (kcol < rows * steps)

    for c in first:
        c.wait_recv()

    second = [[], [], []]
    for t in range(3):
        for pair in range(heads // 2):
            weight_copies[t * (heads // 2) + pair].wait()

        @pl.loop(0, heads // 2)
        def _(pair):
            a = jnp.concatenate([wq[t, 2 * pair], wq[t, 2 * pair + 1]], axis=1)
            lhs = xg[...].reshape(ndp * TILE, feats)
            r = jnp.dot(lhs, a, preferred_element_type=f32)
            raw[2 * pair] = r[:, :hd].reshape(ndp, TILE, hd)
            raw[2 * pair + 1] = r[:, hd:].reshape(ndp, TILE, hd)

        for j in range(caps):
            acc = jnp.where((rank_rows[j] == j)[None], raw[j], 0.0)
            for h in range(j + 1, j + spare + 1):
                acc = jnp.where((rank_rows[h] == j)[None], raw[h], acc)
            packed[t, :, :, j * hd : (j + 1) * hd] = acc
            psend[t, :, :, j * hd : (j + 1) * hd] = acc.astype(bf16)
        for k in range(1, ndp):
            i = t * (ndp - 1) + k - 1
            c = dp_copy(k, psend.at[t, lax.rem(me + k, ndp)], precv.at[t, me], s2.at[i], r2.at[i])
            c.start()
            second[t].append(c)

    by_head = []
    for t in range(3):
        acc = packed[t, me]
        for k in range(1, ndp):
            second[t][k - 1].wait_recv()
            acc = acc + precv[t, lax.rem(me + ndp - k, ndp)].astype(f32)
        part = []
        for h in range(heads):
            v = jnp.zeros((TILE, hd), f32)
            for j in range(max(0, h - spare), min(caps, h + 1)):
                v = jnp.where(rank_rows[h] == j, acc[:, j * hd : (j + 1) * hd], v)
            part.append(v.astype(bf16))
        by_head.append(part)

    late[0].wait()
    late[1].wait()
    scale = hd ** (-0.5)
    nt_dims = (((1,), (1,)), ((), ()))
    for h in range(heads):
        q, kn, vn = by_head[0][h], by_head[1][h], by_head[2][h]
        wide = lax.dot_general(
            q, kc[:, h].reshape(rows * cache, hd), nt_dims, preferred_element_type=f32
        )
        old = wide[:, :cache]
        for r in range(1, rows):
            old = jnp.where(row_is[r], wide[:, r * cache : (r + 1) * cache], old)
        old = old * scale
        new = lax.dot_general(q, kn, nt_dims, preferred_element_type=f32) * scale
        alive = jnp.zeros((TILE, TILE), jnp.int32)
        for s in range(steps):
            alive = jnp.where((kcol >= rows * s) & (kcol < rows * (s + 1)), live[s][h], alive)
        new_valid = same & (alive > 0)
        top = jnp.maximum(
            jnp.max(jnp.where(old_valid, old, -jnp.inf), axis=1, keepdims=True),
            jnp.max(jnp.where(new_valid, new, -jnp.inf), axis=1, keepdims=True),
        )
        old_w = jnp.where(old_valid, jnp.exp(old - top), 0.0)
        new_w = jnp.where(new_valid, jnp.exp(new - top), 0.0)
        norm = jnp.sum(old_w, axis=1, keepdims=True) + jnp.sum(new_w, axis=1, keepdims=True)
        old_p = old_w / norm
        new_p = (new_w / norm).astype(bf16)
        spread_p = jnp.concatenate(
            [jnp.where(row_is[r], old_p, 0.0).astype(bf16) for r in range(rows)], axis=1
        )
        mixed = jnp.dot(
            spread_p, vc[:, h].reshape(rows * cache, hd), preferred_element_type=f32
        ) + jnp.dot(new_p, vn, preferred_element_type=f32)
        mixed = jnp.where(rank_rows[h] >= 0, mixed, 0.0)
        mg[me, :, h * hd : (h + 1) * hd] = mixed.astype(bf16)
    third = []
    for k in range(1, ndp):
        c = dp_copy(k, mg.at[me], mg.at[me], s3.at[k - 1], r3.at[k - 1])
        c.start()
        third.append(c)
    late[2].wait()
    for c in third:
        c.wait_recv()

    gathered = mg[...].reshape(ndp * TILE, heads * hd)
    lhs = jnp.dot(perm_ref[...], gathered, preferred_element_type=f32).astype(bf16)
    if direct:
        cols = feats // nt

        def block(c):
            w = wo[:, :, pl.ds(pl.multiple_of(c * cols, cols), cols)].reshape(heads * hd, cols)
            return jnp.dot(lhs, w, preferred_element_type=f32)

        fourth = []
        order = [nt // 2] + [k for k in range(1, nt) if k != nt // 2]
        for k in order:
            peer = lax.rem(mt + k, nt)
            osend[k - 1] = block(peer).astype(bf16)
            c = pltpu.make_async_remote_copy(
                src_ref=osend.at[k - 1],
                dst_ref=orecv.at[k - 1],
                send_sem=s4.at[k - 1],
                recv_sem=r4.at[k - 1],
                device_id={"tensor": peer},
                device_id_type=MESH,
            )
            c.start()
            fourth.append((k, c))
        acc = block(mt)
        for k, c in reversed(fourth):
            c.wait_recv()
            acc = acc + orecv[k - 1].astype(f32)
        out_ref[...] = acc.astype(out_ref.dtype)
        for k, c in fourth:
            c.wait_send()
    else:
        out_ref[...] = jnp.dot(
            lhs, wo[...].reshape(heads * hd, feats), preferred_element_type=f32
        )
    for c in first + second[0] + second[1] + second[2] + third:
        c.wait_send()


def body(inputs, ln_gain, w_qkv, w_out, key_cache, value_cache, cache_lens, active_heads):
    steps, rows, total = inputs.shape
    heads, feats, hd = w_qkv.shape[1:]
    ndp, nt = lax.axis_size("dp"), lax.axis_size("tensor")
    direct = (feats // nt) % 128 == 0
    count = steps * ndp * rows
    perm = np.zeros((count, ndp * TILE), np.float32)
    for s in range(steps):
        for p in range(ndp):
            for r in range(rows):
                perm[(s * ndp + p) * rows + r, p * TILE + s * rows + r] = 1.0
    bf16, f32 = jnp.bfloat16, jnp.float32
    cols = feats // nt if direct else 128
    orows = count if direct else TILE
    vmem = pl.BlockSpec(memory_space=pltpu.VMEM)
    smem = pl.BlockSpec(memory_space=pltpu.SMEM)
    hbm = pl.BlockSpec(memory_space=pl.ANY)
    dma = pltpu.SemaphoreType.DMA
    out = pl.pallas_call(
        functools.partial(kernel, (ndp, nt, heads, steps, rows, direct)),
        out_shape=jax.ShapeDtypeStruct((count, cols if direct else feats), bf16 if direct else f32),
        in_specs=[vmem, vmem, vmem, smem, smem, hbm, hbm, hbm, hbm],
        out_specs=vmem,
        scratch_shapes=[
            pltpu.VMEM(w_qkv.shape, bf16),
            pltpu.VMEM(w_out.shape, bf16),
            pltpu.VMEM(key_cache.shape, bf16),
            pltpu.VMEM(value_cache.shape, bf16),
            pltpu.VMEM((TILE, total), f32),
            pltpu.VMEM((ndp, TILE, feats), bf16),
            pltpu.VMEM((ndp, TILE, feats), bf16),
            pltpu.VMEM((heads, ndp, TILE, hd), f32),
            pltpu.VMEM((3, ndp, TILE, HEAD_CAP * hd), f32),
            pltpu.VMEM((3, ndp, TILE, HEAD_CAP * hd), bf16),
            pltpu.VMEM((3, ndp, TILE, HEAD_CAP * hd), bf16),
            pltpu.VMEM((ndp, TILE, heads * hd), bf16),
            pltpu.VMEM((nt - 1, orows, cols), bf16),
            pltpu.VMEM((nt - 1, orows, cols), bf16),
            dma((3 * (heads // 2),)),
            dma((3,)),
            dma((ndp - 1,)),
            dma((ndp - 1,)),
            dma((3 * (ndp - 1),)),
            dma((3 * (ndp - 1),)),
            dma((ndp - 1,)),
            dma((ndp - 1,)),
            dma((nt - 1,)),
            dma((nt - 1,)),
        ],
        compiler_params=pltpu.CompilerParams(
            collective_id=0, has_side_effects=True, vmem_limit_bytes=56 * 1024 * 1024
        ),
    )(
        inputs,
        ln_gain.reshape(1, total),
        jnp.asarray(perm, bf16),
        cache_lens,
        active_heads,
        w_qkv,
        w_out,
        key_cache,
        value_cache,
    )
    if not direct:
        out = lax.psum_scatter(out, "tensor", scatter_dimension=1, tiled=True).astype(bf16)
    return out.reshape(steps, ndp * rows, -1)


def solution(mesh):
    placed = (
        P(None, ("groups", "dp"), None),
        P(),
        P(None, "tensor", "dp", None),
        P("tensor", None, "dp"),
        P(("groups", "dp"), "tensor", None, None),
        P(("groups", "dp"), "tensor", None, None),
        P(("groups", "dp")),
        P("groups", None),
    )
    return jax.shard_map(
        body,
        mesh=mesh,
        in_specs=placed,
        out_specs=P(None, "groups", ("dp", "tensor")),
        check_vma=False,
    )
```

```python
import functools

import jax
import jax.numpy as jnp
import numpy as np
from jax import lax
from jax.experimental import pallas as pl
from jax.experimental.pallas import tpu as pltpu
from jax.sharding import PartitionSpec as P

HEAD_CAP = 4
TILE = 16
MESH = pl.DeviceIdType.MESH


def kernel(
    dims,
    x_ref,
    gain_ref,
    perm_ref,
    lens_ref,
    active_ref,
    wqkv_hbm,
    wout_hbm,
    kc_hbm,
    vc_hbm,
    out_ref,
    wq,
    wo,
    kc,
    vc,
    rows32,
    nsend,
    xg,
    raw,
    packed,
    psend,
    precv,
    mg,
    osend,
    orecv,
    w_sem,
    c_sem,
    s1,
    r1,
    s2,
    r2,
    s3,
    r3,
    s4,
    r4,
    s5,
    r5,
):
    ndp, nt, heads, steps, rows, direct = dims
    hd = wq.shape[3]
    feats = wq.shape[2]
    cache = kc.shape[2]
    caps = HEAD_CAP
    spare = heads - caps
    me = lax.axis_index("dp")
    mt = lax.axis_index("tensor")
    f32, bf16 = jnp.float32, jnp.bfloat16

    weight_copies = []
    for t in range(3):
        for pair in range(heads // 2):
            c = pltpu.make_async_copy(
                wqkv_hbm.at[t, pl.ds(2 * pair, 2)],
                wq.at[t, pl.ds(2 * pair, 2)],
                w_sem.at[t * (heads // 2) + pair],
            )
            c.start()
            weight_copies.append(c)
    late = [
        pltpu.make_async_copy(kc_hbm, kc, c_sem.at[0]),
        pltpu.make_async_copy(vc_hbm, vc, c_sem.at[1]),
        pltpu.make_async_copy(wout_hbm, wo, c_sem.at[2]),
    ]
    for c in late:
        c.start()

    barrier = pltpu.get_barrier_semaphore()
    for k in range(1, ndp):
        pl.semaphore_signal(
            barrier, inc=1, device_id={"dp": lax.rem(me + k, ndp)}, device_id_type=MESH
        )
    if direct:
        for k in range(1, nt):
            pl.semaphore_signal(
                barrier, inc=1, device_id={"tensor": lax.rem(mt + k, nt)}, device_id_type=MESH
            )

    total = x_ref.shape[2]
    if TILE > steps * rows:
        rows32[...] = jnp.zeros_like(rows32)
    for s in range(steps):
        v = x_ref[s].astype(f32)
        center = v - jnp.sum(v, axis=-1, keepdims=True) * (1.0 / total)
        spread = jnp.sum(center * center, axis=-1, keepdims=True) * (1.0 / total)
        rows32[rows * s : rows * (s + 1), :] = center * lax.rsqrt(spread + 1e-05) * gain_ref[...]
    halves, _, _, width = xg.shape
    core = lax.rem(mt, 2)
    sibling = mt + 1 - 2 * core
    mine = core if halves == 2 else 0

    def columns(p, half):
        return rows32[:, pl.ds(pl.multiple_of(p * feats + half * width, 128), width)].astype(bf16)

    for k in range(1, ndp):
        nsend[k - 1] = columns(lax.rem(me + k, ndp), mine)

    pl.semaphore_wait(barrier, ndp - 1 + (nt - 1 if direct else 0))

    def dp_copy(k, src, dst, send, recv):
        return pltpu.make_async_remote_copy(
            src_ref=src,
            dst_ref=dst,
            send_sem=send,
            recv_sem=recv,
            device_id={"dp": lax.rem(me + k, ndp)},
            device_id_type=MESH,
        )

    first = []
    for k in range(1, ndp):
        c = dp_copy(k, nsend.at[k - 1], xg.at[mine, me], s1.at[k - 1], r1.at[k - 1])
        c.start()
        first.append(c)
    for half in range(halves):
        xg[half, me] = columns(me, half)

    row = lax.broadcasted_iota(jnp.int32, (TILE, hd), 0)
    step_is = [(row >= rows * s) & (row < rows * (s + 1)) for s in range(steps)]
    row_is = []
    for r in range(rows):
        m = row == r
        for s in range(1, steps):
            m = m | (row == rows * s + r)
        row_is.append(m)
    live = []
    slot_of = []
    for s in range(steps):
        ids = [active_ref[s, a] for a in range(active_ref.shape[1])]
        flags, ranks = [], []
        seen = jnp.int32(0)
        for h in range(heads):
            hid = mt * heads + h
            f = jnp.int32(0)
            for i in ids:
                f = f + jnp.where(i == hid, jnp.int32(1), jnp.int32(0))
            flags.append(f)
            ranks.append(jnp.where(f > 0, jnp.maximum(seen, h - spare), jnp.int32(-1)))
            seen = seen + f
        live.append(flags)
        slot_of.append(ranks)
    rank_rows = []
    for h in range(heads):
        v = jnp.full((TILE, hd), -1, jnp.int32)
        for s in range(steps):
            v = jnp.where(step_is[s], slot_of[s][h], v)
        rank_rows.append(v)
    len_rows = jnp.full((TILE, cache), cache, jnp.int32)
    for r in range(rows):
        len_rows = jnp.where(row_is[r], lens_ref[r], len_rows)
    old_valid = lax.broadcasted_iota(jnp.int32, (TILE, cache), 1) < len_rows
    qrow = lax.broadcasted_iota(jnp.int32, (TILE, TILE), 0)
    kcol = lax.broadcasted_iota(jnp.int32, (TILE, TILE), 1)
    same = qrow == kcol
    for d in range(1, steps):
        same = same | (qrow - kcol == rows * d)
    same = same & (kcol < rows * steps)

    shared = []
    for k in range(1, ndp):
        first[k - 1].wait_recv()
        if halves == 2:
            piece = xg.at[core, lax.rem(me + ndp - k, ndp)]
            c = pltpu.make_async_remote_copy(
                src_ref=piece,
                dst_ref=piece,
                send_sem=s5.at[k - 1],
                recv_sem=r5.at[k - 1],
                device_id={"tensor": sibling},
                device_id_type=MESH,
            )
            c.start()
            shared.append(c)

    def project(t, pair, half):
        depth = pl.ds(pl.multiple_of(half * width, 128), width)
        a = jnp.concatenate([wq[t, 2 * pair, depth], wq[t, 2 * pair + 1, depth]], axis=1)
        lhs = xg[half].reshape(ndp * TILE, width)
        return jnp.dot(lhs, a, preferred_element_type=f32)

    def keep(pair, r):
        raw[2 * pair] = r[:, :hd].reshape(ndp, TILE, hd)
        raw[2 * pair + 1] = r[:, hd:].reshape(ndp, TILE, hd)

    second = [[], [], []]
    for t in range(3):
        for pair in range(heads // 2):
            weight_copies[t * (heads // 2) + pair].wait()

        if t == 0 and halves == 2:

            @pl.loop(0, heads // 2)
            def _(pair):
                keep(pair, project(t, pair, core))

            for c in shared:
                c.wait_recv()

            @pl.loop(0, heads // 2)
            def _(pair):
                r = project(t, pair, 1 - core)
                keep(
                    pair,
                    r
                    + jnp.concatenate(
                        [raw[2 * pair + i].reshape(ndp * TILE, hd) for i in range(2)], axis=1
                    ),
                )
        else:

            @pl.loop(0, heads // 2)
            def _(pair):
                r = project(t, pair, 0)
                for half in range(1, halves):
                    r = r + project(t, pair, half)
                keep(pair, r)

        for j in range(caps):
            acc = jnp.where((rank_rows[j] == j)[None], raw[j], 0.0)
            for h in range(j + 1, j + spare + 1):
                acc = jnp.where((rank_rows[h] == j)[None], raw[h], acc)
            packed[t, :, :, j * hd : (j + 1) * hd] = acc
            psend[t, :, :, j * hd : (j + 1) * hd] = acc.astype(bf16)
        for k in range(1, ndp):
            i = t * (ndp - 1) + k - 1
            c = dp_copy(k, psend.at[t, lax.rem(me + k, ndp)], precv.at[t, me], s2.at[i], r2.at[i])
            c.start()
            second[t].append(c)

    def reduced(t):
        acc = packed[t, me]
        for k in range(1, ndp):
            second[t][k - 1].wait_recv()
            acc = acc + precv[t, lax.rem(me + ndp - k, ndp)].astype(f32)
        part = []
        for h in range(heads):
            v = jnp.zeros((TILE, hd), f32)
            for j in range(max(0, h - spare), min(caps, h + 1)):
                v = jnp.where(rank_rows[h] == j, acc[:, j * hd : (j + 1) * hd], v)
            part.append(v.astype(bf16))
        return part

    late[0].wait()
    late[1].wait()
    queries = reduced(0)
    scale = hd ** (-0.5)
    nt_dims = (((1,), (1,)), ((), ()))
    olds = []
    for h in range(heads):
        wide = lax.dot_general(
            queries[h], kc[:, h].reshape(rows * cache, hd), nt_dims, preferred_element_type=f32
        )
        old = wide[:, :cache]
        for r in range(1, rows):
            old = jnp.where(row_is[r], wide[:, r * cache : (r + 1) * cache], old)
        olds.append(old * scale)
    new_keys = reduced(1)
    probs = []
    for h in range(heads):
        old = olds[h]
        new = lax.dot_general(queries[h], new_keys[h], nt_dims, preferred_element_type=f32) * scale
        alive = jnp.zeros((TILE, TILE), jnp.int32)
        for s in range(steps):
            alive = jnp.where((kcol >= rows * s) & (kcol < rows * (s + 1)), live[s][h], alive)
        new_valid = same & (alive > 0)
        top = jnp.maximum(
            jnp.max(jnp.where(old_valid, old, -jnp.inf), axis=1, keepdims=True),
            jnp.max(jnp.where(new_valid, new, -jnp.inf), axis=1, keepdims=True),
        )
        old_w = jnp.where(old_valid, jnp.exp(old - top), 0.0)
        new_w = jnp.where(new_valid, jnp.exp(new - top), 0.0)
        norm = jnp.sum(old_w, axis=1, keepdims=True) + jnp.sum(new_w, axis=1, keepdims=True)
        old_p = old_w / norm
        new_p = (new_w / norm).astype(bf16)
        spread_p = jnp.concatenate(
            [jnp.where(row_is[r], old_p, 0.0).astype(bf16) for r in range(rows)], axis=1
        )
        cached = jnp.dot(
            spread_p, vc[:, h].reshape(rows * cache, hd), preferred_element_type=f32
        )
        probs.append((cached, new_p))
    new_values = reduced(2)
    mixed = []
    for h in range(heads):
        cached, new_p = probs[h]
        mixed.append(cached + jnp.dot(new_p, new_values[h], preferred_element_type=f32))
    for j in range(caps):
        acc = jnp.where(rank_rows[j] == j, mixed[j], 0.0)
        for h in range(j + 1, j + spare + 1):
            acc = jnp.where(rank_rows[h] == j, mixed[h], acc)
        mg[me, :, j * hd : (j + 1) * hd] = acc.astype(bf16)
    third = []
    for k in range(1, ndp):
        c = dp_copy(k, mg.at[me], mg.at[me], s3.at[k - 1], r3.at[k - 1])
        c.start()
        third.append(c)
    late[2].wait()
    for c in third:
        c.wait_recv()

    gathered = mg[...].reshape(ndp * TILE, caps * hd)
    ordered = jnp.dot(perm_ref[...], gathered, preferred_element_type=f32)
    group = ndp * rows
    by_step = []
    for s in range(steps):
        here = ordered[s * group : (s + 1) * group]
        part = []
        for h in range(heads):
            slot = jnp.full((group, hd), slot_of[s][h], jnp.int32)
            v = jnp.zeros((group, hd), f32)
            for j in range(max(0, h - spare), min(caps, h + 1)):
                v = jnp.where(slot == j, here[:, j * hd : (j + 1) * hd], v)
            part.append(v)
        by_step.append(jnp.concatenate(part, axis=1))
    lhs = jnp.concatenate(by_step, axis=0).astype(bf16)
    if direct:
        cols = feats // nt

        def block(c):
            w = wo[:, :, pl.ds(pl.multiple_of(c * cols, cols), cols)].reshape(heads * hd, cols)
            return jnp.dot(lhs, w, preferred_element_type=f32)

        fourth = []
        partners = []
        for k in range(2, nt, 2):
            partners += [lax.rem(mt + k, nt), lax.rem(sibling + k, nt)]
        partners.append(sibling)
        for k, peer in enumerate(partners, 1):
            osend[k - 1] = block(peer).astype(bf16)
            c = pltpu.make_async_remote_copy(
                src_ref=osend.at[k - 1],
                dst_ref=orecv.at[k - 1],
                send_sem=s4.at[k - 1],
                recv_sem=r4.at[k - 1],
                device_id={"tensor": peer},
                device_id_type=MESH,
            )
            c.start()
            fourth.append((k, c))
        acc = block(mt)
        for k, c in reversed(fourth):
            c.wait_recv()
            acc = acc + orecv[k - 1].astype(f32)
        out_ref[...] = acc.astype(out_ref.dtype)
        for k, c in fourth:
            c.wait_send()
    else:
        out_ref[...] = jnp.dot(
            lhs, wo[...].reshape(heads * hd, feats), preferred_element_type=f32
        )
    for c in first + shared + second[0] + second[1] + second[2] + third:
        c.wait_send()


def body(inputs, ln_gain, w_qkv, w_out, key_cache, value_cache, cache_lens, active_heads):
    steps, rows, total = inputs.shape
    heads, feats, hd = w_qkv.shape[1:]
    ndp, nt = lax.axis_size("dp"), lax.axis_size("tensor")
    direct = (feats // nt) % 128 == 0
    halves = 2 if direct and (feats // 2) % 128 == 0 else 1
    count = steps * ndp * rows
    perm = np.zeros((count, ndp * TILE), np.float32)
    for s in range(steps):
        for p in range(ndp):
            for r in range(rows):
                perm[(s * ndp + p) * rows + r, p * TILE + s * rows + r] = 1.0
    bf16, f32 = jnp.bfloat16, jnp.float32
    cols = feats // nt if direct else 128
    orows = count if direct else TILE
    vmem = pl.BlockSpec(memory_space=pltpu.VMEM)
    smem = pl.BlockSpec(memory_space=pltpu.SMEM)
    hbm = pl.BlockSpec(memory_space=pl.ANY)
    dma = pltpu.SemaphoreType.DMA
    out = pl.pallas_call(
        functools.partial(kernel, (ndp, nt, heads, steps, rows, direct)),
        out_shape=jax.ShapeDtypeStruct((count, cols if direct else feats), bf16 if direct else f32),
        in_specs=[vmem, vmem, vmem, smem, smem, hbm, hbm, hbm, hbm],
        out_specs=vmem,
        scratch_shapes=[
            pltpu.VMEM(w_qkv.shape, bf16),
            pltpu.VMEM(w_out.shape, bf16),
            pltpu.VMEM(key_cache.shape, bf16),
            pltpu.VMEM(value_cache.shape, bf16),
            pltpu.VMEM((TILE, total), f32),
            pltpu.VMEM((ndp - 1, TILE, feats // halves), bf16),
            pltpu.VMEM((halves, ndp, TILE, feats // halves), bf16),
            pltpu.VMEM((heads, ndp, TILE, hd), f32),
            pltpu.VMEM((3, ndp, TILE, HEAD_CAP * hd), f32),
            pltpu.VMEM((3, ndp, TILE, HEAD_CAP * hd), bf16),
            pltpu.VMEM((3, ndp, TILE, HEAD_CAP * hd), bf16),
            pltpu.VMEM((ndp, TILE, HEAD_CAP * hd), bf16),
            pltpu.VMEM((nt - 1, orows, cols), bf16),
            pltpu.VMEM((nt - 1, orows, cols), bf16),
            dma((3 * (heads // 2),)),
            dma((3,)),
            dma((ndp - 1,)),
            dma((ndp - 1,)),
            dma((3 * (ndp - 1),)),
            dma((3 * (ndp - 1),)),
            dma((ndp - 1,)),
            dma((ndp - 1,)),
            dma((nt - 1,)),
            dma((nt - 1,)),
            dma((ndp - 1,)),
            dma((ndp - 1,)),
        ],
        compiler_params=pltpu.CompilerParams(
            collective_id=0, has_side_effects=True, vmem_limit_bytes=56 * 1024 * 1024
        ),
    )(
        inputs,
        ln_gain.reshape(1, total),
        jnp.asarray(perm, bf16),
        cache_lens,
        active_heads,
        w_qkv,
        w_out,
        key_cache,
        value_cache,
    )
    if not direct:
        out = lax.psum_scatter(out, "tensor", scatter_dimension=1, tiled=True).astype(bf16)
    return out.reshape(steps, ndp * rows, -1)


def solution(mesh):
    placed = (
        P(None, ("groups", "dp"), None),
        P(),
        P(None, "tensor", "dp", None),
        P("tensor", None, "dp"),
        P(("groups", "dp"), "tensor", None, None),
        P(("groups", "dp"), "tensor", None, None),
        P(("groups", "dp")),
        P("groups", None),
    )
    return jax.shard_map(
        body,
        mesh=mesh,
        in_specs=placed,
        out_specs=P(None, "groups", ("dp", "tensor")),
        check_vma=False,
    )
```

```python
import functools

import jax
import jax.numpy as jnp
import numpy as np
from jax import lax
from jax.experimental import pallas as pl
from jax.experimental.pallas import tpu as pltpu
from jax.sharding import PartitionSpec as P

HEAD_CAP = 4
TILE = 16
MESH = pl.DeviceIdType.MESH


def kernel(
    dims,
    x_ref,
    gain_ref,
    perm_ref,
    lens_ref,
    active_ref,
    wqkv_hbm,
    wout_hbm,
    kc_hbm,
    vc_hbm,
    out_ref,
    wq,
    wo,
    kc,
    vc,
    rows32,
    nsend,
    xg,
    raw,
    packed,
    psend,
    precv,
    mg,
    osend,
    orecv,
    w_sem,
    c_sem,
    s1,
    r1,
    s2,
    r2,
    s3,
    r3,
    s4,
    r4,
    s5,
    r5,
):
    ndp, nt, heads, steps, rows, direct = dims
    hd = wq.shape[3]
    feats = wq.shape[2]
    cache = kc.shape[2]
    caps = HEAD_CAP
    spare = heads - caps
    me = lax.axis_index("dp")
    mt = lax.axis_index("tensor")
    f32, bf16 = jnp.float32, jnp.bfloat16

    weight_copies = []
    for t in range(3):
        for pair in range(heads // 2):
            c = pltpu.make_async_copy(
                wqkv_hbm.at[t, pl.ds(2 * pair, 2)],
                wq.at[t, pl.ds(2 * pair, 2)],
                w_sem.at[t * (heads // 2) + pair],
            )
            c.start()
            weight_copies.append(c)
    late = [
        pltpu.make_async_copy(kc_hbm, kc, c_sem.at[0]),
        pltpu.make_async_copy(vc_hbm, vc, c_sem.at[1]),
        pltpu.make_async_copy(wout_hbm, wo, c_sem.at[2]),
    ]
    for c in late:
        c.start()

    barrier = pltpu.get_barrier_semaphore()
    for k in range(1, ndp):
        pl.semaphore_signal(
            barrier, inc=1, device_id={"dp": lax.rem(me + k, ndp)}, device_id_type=MESH
        )
    if direct:
        for k in range(1, nt):
            pl.semaphore_signal(
                barrier, inc=1, device_id={"tensor": lax.rem(mt + k, nt)}, device_id_type=MESH
            )

    total = x_ref.shape[2]
    if TILE > steps * rows:
        rows32[...] = jnp.zeros_like(rows32)
    for s in range(steps):
        v = x_ref[s].astype(f32)
        center = v - jnp.sum(v, axis=-1, keepdims=True) * (1.0 / total)
        spread = jnp.sum(center * center, axis=-1, keepdims=True) * (1.0 / total)
        rows32[rows * s : rows * (s + 1), :] = center * lax.rsqrt(spread + 1e-05) * gain_ref[...]
    halves, _, _, width = xg.shape
    core = lax.rem(mt, 2)
    sibling = mt + 1 - 2 * core
    mine = core if halves == 2 else 0

    def columns(p, half):
        return rows32[:, pl.ds(pl.multiple_of(p * feats + half * width, 128), width)].astype(bf16)

    for k in range(1, ndp):
        nsend[k - 1] = columns(lax.rem(me + k, ndp), mine)

    pl.semaphore_wait(barrier, ndp - 1 + (nt - 1 if direct else 0))

    def dp_copy(k, src, dst, send, recv):
        return pltpu.make_async_remote_copy(
            src_ref=src,
            dst_ref=dst,
            send_sem=send,
            recv_sem=recv,
            device_id={"dp": lax.rem(me + k, ndp)},
            device_id_type=MESH,
        )

    first = []
    for k in range(1, ndp):
        c = dp_copy(k, nsend.at[k - 1], xg.at[mine, me], s1.at[k - 1], r1.at[k - 1])
        c.start()
        first.append(c)
    for half in range(halves):
        xg[half, me] = columns(me, half)

    row = lax.broadcasted_iota(jnp.int32, (TILE, hd), 0)
    step_is = [(row >= rows * s) & (row < rows * (s + 1)) for s in range(steps)]
    row_is = []
    for r in range(rows):
        m = row == r
        for s in range(1, steps):
            m = m | (row == rows * s + r)
        row_is.append(m)
    live = []
    slot_of = []
    for s in range(steps):
        ids = [active_ref[s, a] for a in range(active_ref.shape[1])]
        flags, ranks = [], []
        seen = jnp.int32(0)
        for h in range(heads):
            hid = mt * heads + h
            f = jnp.int32(0)
            for i in ids:
                f = f + jnp.where(i == hid, jnp.int32(1), jnp.int32(0))
            flags.append(f)
            ranks.append(jnp.where(f > 0, jnp.maximum(seen, h - spare), jnp.int32(-1)))
            seen = seen + f
        live.append(flags)
        slot_of.append(ranks)
    rank_rows = []
    for h in range(heads):
        v = jnp.full((TILE, hd), -1, jnp.int32)
        for s in range(steps):
            v = jnp.where(step_is[s], slot_of[s][h], v)
        rank_rows.append(v)
    len_rows = jnp.full((TILE, cache), cache, jnp.int32)
    for r in range(rows):
        len_rows = jnp.where(row_is[r], lens_ref[r], len_rows)
    old_valid = lax.broadcasted_iota(jnp.int32, (TILE, cache), 1) < len_rows
    qrow = lax.broadcasted_iota(jnp.int32, (TILE, TILE), 0)
    kcol = lax.broadcasted_iota(jnp.int32, (TILE, TILE), 1)
    same = qrow == kcol
    for d in range(1, steps):
        same = same | (qrow - kcol == rows * d)
    same = same & (kcol < rows * steps)

    shared = []
    for k in range(1, ndp):
        first[k - 1].wait_recv()
        if halves == 2:
            piece = xg.at[core, lax.rem(me + ndp - k, ndp)]
            c = pltpu.make_async_remote_copy(
                src_ref=piece,
                dst_ref=piece,
                send_sem=s5.at[k - 1],
                recv_sem=r5.at[k - 1],
                device_id={"tensor": sibling},
                device_id_type=MESH,
            )
            c.start()
            shared.append(c)

    def project(t, pair, half):
        depth = pl.ds(pl.multiple_of(half * width, 128), width)
        a = jnp.concatenate([wq[t, 2 * pair, depth], wq[t, 2 * pair + 1, depth]], axis=1)
        lhs = xg[half].reshape(ndp * TILE, width)
        return jnp.dot(lhs, a, preferred_element_type=f32)

    def keep(pair, r):
        raw[2 * pair] = r[:, :hd].reshape(ndp, TILE, hd)
        raw[2 * pair + 1] = r[:, hd:].reshape(ndp, TILE, hd)

    second = [[], [], []]
    for t in range(3):
        for pair in range(heads // 2):
            weight_copies[t * (heads // 2) + pair].wait()

        if t == 0 and halves == 2:

            for pair in range(heads // 2):
                keep(pair, project(t, pair, core))

            for c in shared:
                c.wait_recv()

            for pair in range(heads // 2):
                r = project(t, pair, 1 - core)
                keep(
                    pair,
                    r
                    + jnp.concatenate(
                        [raw[2 * pair + i].reshape(ndp * TILE, hd) for i in range(2)], axis=1
                    ),
                )
        else:

            for pair in range(heads // 2):
                r = project(t, pair, 0)
                for half in range(1, halves):
                    r = r + project(t, pair, half)
                keep(pair, r)

        for j in range(caps):
            acc = jnp.where((rank_rows[j] == j)[None], raw[j], 0.0)
            for h in range(j + 1, j + spare + 1):
                acc = jnp.where((rank_rows[h] == j)[None], raw[h], acc)
            packed[t, :, :, j * hd : (j + 1) * hd] = acc
            psend[t, :, :, j * hd : (j + 1) * hd] = acc.astype(bf16)
        for k in range(1, ndp):
            i = t * (ndp - 1) + k - 1
            c = dp_copy(k, psend.at[t, lax.rem(me + k, ndp)], precv.at[t, me], s2.at[i], r2.at[i])
            c.start()
            second[t].append(c)

    def reduced(t):
        acc = packed[t, me]
        for k in range(1, ndp):
            second[t][k - 1].wait_recv()
            acc = acc + precv[t, lax.rem(me + ndp - k, ndp)].astype(f32)
        part = []
        for h in range(heads):
            v = jnp.zeros((TILE, hd), f32)
            for j in range(max(0, h - spare), min(caps, h + 1)):
                v = jnp.where(rank_rows[h] == j, acc[:, j * hd : (j + 1) * hd], v)
            part.append(v.astype(bf16))
        return part

    late[0].wait()
    late[1].wait()
    queries = reduced(0)
    scale = hd ** (-0.5)
    nt_dims = (((1,), (1,)), ((), ()))
    olds = []
    for h in range(heads):
        wide = lax.dot_general(
            queries[h], kc[:, h].reshape(rows * cache, hd), nt_dims, preferred_element_type=f32
        )
        old = wide[:, :cache]
        for r in range(1, rows):
            old = jnp.where(row_is[r], wide[:, r * cache : (r + 1) * cache], old)
        olds.append(old * scale)
    new_keys = reduced(1)
    probs = []
    for h in range(heads):
        old = olds[h]
        new = lax.dot_general(queries[h], new_keys[h], nt_dims, preferred_element_type=f32) * scale
        alive = jnp.zeros((TILE, TILE), jnp.int32)
        for s in range(steps):
            alive = jnp.where((kcol >= rows * s) & (kcol < rows * (s + 1)), live[s][h], alive)
        new_valid = same & (alive > 0)
        top = jnp.maximum(
            jnp.max(jnp.where(old_valid, old, -jnp.inf), axis=1, keepdims=True),
            jnp.max(jnp.where(new_valid, new, -jnp.inf), axis=1, keepdims=True),
        )
        old_w = jnp.where(old_valid, jnp.exp(old - top), 0.0)
        new_w = jnp.where(new_valid, jnp.exp(new - top), 0.0)
        norm = jnp.sum(old_w, axis=1, keepdims=True) + jnp.sum(new_w, axis=1, keepdims=True)
        old_p = old_w / norm
        new_p = (new_w / norm).astype(bf16)
        spread_p = jnp.concatenate(
            [jnp.where(row_is[r], old_p, 0.0).astype(bf16) for r in range(rows)], axis=1
        )
        cached = jnp.dot(
            spread_p, vc[:, h].reshape(rows * cache, hd), preferred_element_type=f32
        )
        probs.append((cached, new_p))
    new_values = reduced(2)
    mixed = []
    for h in range(heads):
        cached, new_p = probs[h]
        mixed.append(cached + jnp.dot(new_p, new_values[h], preferred_element_type=f32))
    for j in range(caps):
        acc = jnp.where(rank_rows[j] == j, mixed[j], 0.0)
        for h in range(j + 1, j + spare + 1):
            acc = jnp.where(rank_rows[h] == j, mixed[h], acc)
        mg[me, :, j * hd : (j + 1) * hd] = acc.astype(bf16)
    third = []
    for k in range(1, ndp):
        c = dp_copy(k, mg.at[me], mg.at[me], s3.at[k - 1], r3.at[k - 1])
        c.start()
        third.append(c)
    late[2].wait()
    for c in third:
        c.wait_recv()

    gathered = mg[...].reshape(ndp * TILE, caps * hd)
    ordered = jnp.dot(perm_ref[...], gathered, preferred_element_type=f32)
    group = ndp * rows
    by_step = []
    for s in range(steps):
        here = ordered[s * group : (s + 1) * group]
        part = []
        for h in range(heads):
            slot = jnp.full((group, hd), slot_of[s][h], jnp.int32)
            v = jnp.zeros((group, hd), f32)
            for j in range(max(0, h - spare), min(caps, h + 1)):
                v = jnp.where(slot == j, here[:, j * hd : (j + 1) * hd], v)
            part.append(v)
        by_step.append(jnp.concatenate(part, axis=1))
    lhs = jnp.concatenate(by_step, axis=0).astype(bf16)
    if direct:
        cols = feats // nt

        def block(c):
            w = wo[:, :, pl.ds(pl.multiple_of(c * cols, cols), cols)].reshape(heads * hd, cols)
            return jnp.dot(lhs, w, preferred_element_type=f32)

        fourth = []
        partners = []
        for k in range(2, nt, 2):
            partners += [lax.rem(mt + k, nt), lax.rem(sibling + k, nt)]
        partners.append(sibling)
        for k, peer in enumerate(partners, 1):
            osend[k - 1] = block(peer).astype(bf16)
            c = pltpu.make_async_remote_copy(
                src_ref=osend.at[k - 1],
                dst_ref=orecv.at[k - 1],
                send_sem=s4.at[k - 1],
                recv_sem=r4.at[k - 1],
                device_id={"tensor": peer},
                device_id_type=MESH,
            )
            c.start()
            fourth.append((k, c))
        acc = block(mt)
        for k, c in reversed(fourth):
            c.wait_recv()
            acc = acc + orecv[k - 1].astype(f32)
        out_ref[...] = acc.astype(out_ref.dtype)
        for k, c in fourth:
            c.wait_send()
    else:
        out_ref[...] = jnp.dot(
            lhs, wo[...].reshape(heads * hd, feats), preferred_element_type=f32
        )
    for c in first + shared + second[0] + second[1] + second[2] + third:
        c.wait_send()


def body(inputs, ln_gain, w_qkv, w_out, key_cache, value_cache, cache_lens, active_heads):
    steps, rows, total = inputs.shape
    heads, feats, hd = w_qkv.shape[1:]
    ndp, nt = lax.axis_size("dp"), lax.axis_size("tensor")
    direct = (feats // nt) % 128 == 0
    halves = 2 if direct and (feats // 2) % 128 == 0 else 1
    count = steps * ndp * rows
    perm = np.zeros((count, ndp * TILE), np.float32)
    for s in range(steps):
        for p in range(ndp):
            for r in range(rows):
                perm[(s * ndp + p) * rows + r, p * TILE + s * rows + r] = 1.0
    bf16, f32 = jnp.bfloat16, jnp.float32
    cols = feats // nt if direct else 128
    orows = count if direct else TILE
    vmem = pl.BlockSpec(memory_space=pltpu.VMEM)
    smem = pl.BlockSpec(memory_space=pltpu.SMEM)
    hbm = pl.BlockSpec(memory_space=pl.ANY)
    dma = pltpu.SemaphoreType.DMA
    out = pl.pallas_call(
        functools.partial(kernel, (ndp, nt, heads, steps, rows, direct)),
        out_shape=jax.ShapeDtypeStruct((count, cols if direct else feats), bf16 if direct else f32),
        in_specs=[vmem, vmem, vmem, smem, smem, hbm, hbm, hbm, hbm],
        out_specs=vmem,
        scratch_shapes=[
            pltpu.VMEM(w_qkv.shape, bf16),
            pltpu.VMEM(w_out.shape, bf16),
            pltpu.VMEM(key_cache.shape, bf16),
            pltpu.VMEM(value_cache.shape, bf16),
            pltpu.VMEM((TILE, total), f32),
            pltpu.VMEM((ndp - 1, TILE, feats // halves), bf16),
            pltpu.VMEM((halves, ndp, TILE, feats // halves), bf16),
            pltpu.VMEM((heads, ndp, TILE, hd), f32),
            pltpu.VMEM((3, ndp, TILE, HEAD_CAP * hd), f32),
            pltpu.VMEM((3, ndp, TILE, HEAD_CAP * hd), bf16),
            pltpu.VMEM((3, ndp, TILE, HEAD_CAP * hd), bf16),
            pltpu.VMEM((ndp, TILE, HEAD_CAP * hd), bf16),
            pltpu.VMEM((nt - 1, orows, cols), bf16),
            pltpu.VMEM((nt - 1, orows, cols), bf16),
            dma((3 * (heads // 2),)),
            dma((3,)),
            dma((ndp - 1,)),
            dma((ndp - 1,)),
            dma((3 * (ndp - 1),)),
            dma((3 * (ndp - 1),)),
            dma((ndp - 1,)),
            dma((ndp - 1,)),
            dma((nt - 1,)),
            dma((nt - 1,)),
            dma((ndp - 1,)),
            dma((ndp - 1,)),
        ],
        compiler_params=pltpu.CompilerParams(
            collective_id=0, has_side_effects=True, vmem_limit_bytes=56 * 1024 * 1024
        ),
    )(
        inputs,
        ln_gain.reshape(1, total),
        jnp.asarray(perm, bf16),
        cache_lens,
        active_heads,
        w_qkv,
        w_out,
        key_cache,
        value_cache,
    )
    if not direct:
        out = lax.psum_scatter(out, "tensor", scatter_dimension=1, tiled=True).astype(bf16)
    return out.reshape(steps, ndp * rows, -1)


def solution(mesh):
    placed = (
        P(None, ("groups", "dp"), None),
        P(),
        P(None, "tensor", "dp", None),
        P("tensor", None, "dp"),
        P(("groups", "dp"), "tensor", None, None),
        P(("groups", "dp"), "tensor", None, None),
        P(("groups", "dp")),
        P("groups", None),
    )
    return jax.shard_map(
        body,
        mesh=mesh,
        in_specs=placed,
        out_specs=P(None, "groups", ("dp", "tensor")),
        check_vma=False,
    )
```
